32 devices in a mesh: occ: 4 (over y, core), vir: 8 (over z, x).
Axes of the slice: x: 2, y: 2, z: 4, core: 2. Of those that a mesh axis runs over, the one named last changes fastest.
Arguments:
- orbitals: bfloat16 [4, 2048, 4096], P('occ', 'vir'), may hold values from -0.75 to 0.75
- eps_occ: bfloat16 [4], P('occ'), may hold values from -2.5 to -0.5
- eps_vir: bfloat16 [2048], P('vir'), may hold values from 0.5 to 3
Outputs:
- density: bfloat16 [4, 2048, 4096], P('occ', 'vir')
The draws below stay inside these ranges and needn't reach their ends.
All inputs are finite; a program needn't handle non-finite values.
Results may differ from the reference program's by a relative error of at most 0.0047.
Values may be sent and summed in bfloat16 or wider, within the bound.
A program may use at most 64 MiB of HBM per device.

```python
import jax
import jax.numpy as jnp
from jax import lax

NAUX = 4096
VIR_DEV = 256
OCC_DEV = 1
BATCH_DEV = 8
REACH = 1
OCC = 4
VIRT = 2048
N_OCC = 4
N_VIR = 8


def shard_levels(own_key, dims, shards, low, largest):
    factor_of, own = 1.0, jax.random.fold_in(own_key, 6)
    for axis_at, shards_of in shards:
        draws = jnp.exp(jax.random.uniform(jax.random.fold_in(own, axis_at), (shards_of,), jnp.float32, low / len(shards), largest / len(shards)))
        factor_of = factor_of * jnp.repeat(draws, dims[axis_at] // shards_of).reshape([-1 if axis == axis_at else 1 for axis in range(len(dims))])
    return factor_of


def centred(own_key, shape, width, bound, split=(), held_as=jnp.bfloat16):
    array = width * jax.random.normal(own_key, shape, jnp.float32)
    if split:
        array = array * shard_levels(own_key, shape, split, -0.22, 0.18)
    return jnp.clip(array, -bound, bound).astype(held_as)


def setup_inputs(seed: int = 0) -> dict:
    arg_keys = jax.random.split(jax.random.key(seed), 4)
    return {
        "orbitals": centred(arg_keys[0], (OCC, VIRT, NAUX), (NAUX ** -0.25), 0.75, ((0, 4), (1, 8))),
        "eps_occ": jnp.clip(-2.5 + 2.0 * jax.random.uniform(arg_keys[1], (OCC,), jnp.float32) ** shard_levels(arg_keys[1], (OCC,), ((0, 4),), -0.2, 0.2), -2.5, -0.5).astype(jnp.bfloat16),
        "eps_vir": jnp.clip(0.5 + 2.5 * jax.random.uniform(arg_keys[2], (VIRT,), jnp.float32) ** shard_levels(arg_keys[2], (VIRT,), ((0, 8),), -0.2, 0.2), 0.5, 3.0).astype(jnp.bfloat16),
    }


def reference(orbitals, eps_occ, eps_vir):
    occ_all, vir_all, aux_width = orbitals.shape
    batch_rows = orbitals.reshape(occ_all, N_VIR, VIR_DEV, aux_width)[:, :, :BATCH_DEV, :]
    batch_rows = batch_rows.reshape(N_OCC, OCC_DEV, N_VIR * BATCH_DEV, aux_width).astype(jnp.float32)
    batch_energy = eps_vir.reshape(N_VIR, VIR_DEV)[:, :BATCH_DEV].reshape(-1).astype(jnp.float32)
    vir_energy = eps_vir.astype(jnp.float32)
    occ_blocks = eps_occ.astype(jnp.float32).reshape(N_OCC, OCC_DEV)
    full = orbitals.reshape(N_OCC, OCC_DEV, vir_all, aux_width)
    offsets = jnp.arange(-REACH, REACH + 1, dtype=jnp.int32)
    highest = lax.Precision.HIGHEST

    def one_block(index):
        partners = ((index + offsets) % N_OCC).astype(jnp.int32)
        resident = full[index].astype(jnp.float32)
        slices = full[partners].astype(jnp.float32)
        row_sets = batch_rows[partners]
        coulomb = jnp.einsum("iap,kjbp->iakjb", resident, row_sets, precision=highest)
        exchange = jnp.einsum("ibp,kjap->iakjb", batch_rows[index], slices, precision=highest)
        denominator = (vir_energy[None, :, None, None, None] + batch_energy[None, None, None, None, :]
                       - occ_blocks[index][:, None, None, None, None]
                       - occ_blocks[partners][None, None, :, :, None])
        amplitude = ((2.0 * coulomb - exchange) / denominator).astype(jnp.bfloat16)
        amplitude = lax.optimization_barrier(amplitude).astype(jnp.float32)
        density = jnp.einsum("iakjb,kjbp->iap", amplitude, row_sets, precision=highest)
        return density.astype(jnp.bfloat16)

    result = lax.map(one_block, jnp.arange(N_OCC, dtype=jnp.int32))
    return result.reshape(occ_all, vir_all, aux_width)
```

```python
import functools

import jax
import jax.numpy as jnp
from jax import lax
from jax.experimental import pallas as pl
from jax.experimental.pallas import tpu as pltpu
from jax.sharding import PartitionSpec as P

BATCH_DEV = 8
MESH = pl.DeviceIdType.MESH


def kernel(n_occ, n_vir, orb, ev_ref, eo_ref, out, a, head, raw, rows, mir_out, mir_in, outb,
           send_sem, recv_sem, local_sem, out_sem):
    f32, bf16 = jnp.float32, jnp.bfloat16
    nz = n_vir // 2
    aux = orb.shape[1]
    half = aux // 2
    cut = half // 2
    b = BATCH_DEV
    block = n_vir * b
    o, v = lax.axis_index("occ"), lax.axis_index("vir")
    z, x, core = v // 2, v % 2, o % 2
    along_x = (o, z * 2 + (1 - x))
    sibling = (o + 1 - 2 * core, v)
    far = ((o - 1 + 2 * core + n_occ) % n_occ, v)

    def along_z(s):
        return (o, ((z - s + nz) % nz) * 2 + x)

    barrier = pltpu.get_barrier_semaphore()
    for dev in [along_x, sibling, far] + [along_z(s) for s in range(1, nz)]:
        pl.semaphore_signal(barrier, inc=1, device_id=dev, device_id_type=MESH)

    get_head = pltpu.make_async_copy(orb.at[pl.ds(0, 16)], head, local_sem.at[0])
    get_a = pltpu.make_async_copy(orb, a, local_sem.at[1])
    get_head.start()
    get_a.start()
    get_head.wait()

    top = head[...].astype(f32)[0:b]
    raw[0, 0, 0, :, 0:half] = jnp.concatenate([top[:, :half], top[:, half:]], axis=0).astype(bf16)
    ev = ev_ref[...].astype(f32)
    lane = lax.broadcasted_iota(jnp.int32, (b, 128), 1)
    row = lax.broadcasted_iota(jnp.int32, (b, 128), 0)
    picked = jnp.where(lane == row, jnp.broadcast_to(ev[:, :128], (b, 128)), 0.0)
    batch_energy = jnp.broadcast_to(jnp.sum(picked, axis=1, keepdims=True), (b, 128))
    occ_energy = jnp.broadcast_to(eo_ref[...].astype(f32), (b, 128))
    raw[0, 0, 0, :, half:] = jnp.concatenate([batch_energy, occ_energy], axis=0).astype(bf16)

    def copy(kind, s, src, dst, dev):
        at = kind * nz + s
        return pltpu.make_async_remote_copy(
            src_ref=src, dst_ref=dst, send_sem=send_sem.at[at], recv_sem=recv_sem.at[at],
            device_id=dev, device_id_type=MESH)

    first, last = pl.ds(0, cut), pl.ds(cut, half + 128 - cut)
    to_z = [None] + [copy(0, s, raw.at[0, 0, 0], raw.at[0, s, 0], along_z(s)) for s in range(1, nz)]
    to_x = [copy(1, s, raw.at[0, s, 0], raw.at[0, s, 1], along_x) for s in range(nz)]
    to_far = [copy(2, s, raw.at[0, s, 0], raw.at[2, s, 0], far) for s in range(nz)]
    to_far_x = [copy(3, s, raw.at[0, s, 1, :, first], raw.at[2, s, 1, :, first], far) for s in range(nz)]
    far_to_x = [copy(4, s, raw.at[2, s, 0, :, last], raw.at[2, s, 1, :, last], along_x) for s in range(nz)]
    to_sib = [copy(5, s, raw.at[0, s, 0], raw.at[1, s, 0], sibling) for s in range(nz)]
    to_sib_x = [copy(6, s, raw.at[0, s, 1], raw.at[1, s, 1], sibling) for s in range(nz)]
    mirrors = [copy(7, q, mir_out.at[q], mir_in.at[q], dev) for q, dev in enumerate((sibling, far))]

    def unpack(q, s):
        p0 = raw[q, s, 0, :, 0:half].astype(f32)
        p1 = raw[q, s, 1, :, 0:half].astype(f32)
        at = pl.ds(q * block + s * 2 * b, 2 * b)
        rows[at, 0:half] = jnp.concatenate([p0[0:b], p1[0:b]], axis=0).astype(bf16)
        rows[at, half:] = jnp.concatenate([p0[b:], p1[b:]], axis=0).astype(bf16)

    pl.semaphore_wait(barrier, nz + 2)
    to_x[0].start()
    to_far[0].start()
    for s in range(1, nz):
        to_z[s].start()
    to_sib[0].start()
    for s in range(nz):
        if s + 1 < nz:
            to_z[s + 1].wait_recv()
            to_x[s + 1].start()
            to_far[s + 1].start()
            to_sib[s + 1].start()
        to_x[s].wait_recv()
        to_far_x[s].start()
        to_sib_x[s].start()
        to_far[s].wait_recv()
        far_to_x[s].start()
        unpack(0, s)
    get_a.wait()
    for s in range(nz):
        to_sib[s].wait_recv()
        to_sib_x[s].wait_recv()
        unpack(1, s)
    for s in range(nz):
        to_far_x[s].wait_recv()
        far_to_x[s].wait_recv()
        unpack(2, s)

    def coulomb_of(start, size):
        return lax.dot_general(rows[pl.ds(start, size), :], a[...], (((1,), (1,)), ((), ())),
                               preferred_element_type=f32)

    others = coulomb_of(block, 2 * block)
    for q in range(2):
        mir_out[q] = others[q * block:(q + 1) * block].astype(bf16)
        mirrors[q].start()
    own = coulomb_of(0, block)

    levels = jnp.concatenate([raw[0, s, t, :, half:].astype(f32)[0:b] for s in range(nz) for t in range(2)], axis=0)
    width = a.shape[0]
    reps = width // 128
    levels = jnp.concatenate([levels] * reps, axis=1)
    own_occ = raw[0, 0, 0, :, half:].astype(f32)[b:b + 1]
    base = ev + levels - jnp.concatenate([own_occ] * reps, axis=1)

    def amplitude_of(q, numerator):
        occ = raw[q, 0, 0, :, half:].astype(f32)[b:b + 1]
        return (numerator / (base - jnp.concatenate([occ] * reps, axis=1))).astype(bf16)

    parts = [amplitude_of(0, 2.0 * own - own)]
    for q in range(2):
        mirrors[q].wait_recv()
        parts.append(amplitude_of(q + 1, 2.0 * others[q * block:(q + 1) * block] - mir_in[q].astype(f32)))
    amplitude = jnp.concatenate(parts, axis=0).T

    chunk = outb.shape[2]
    for c in range(aux // chunk):
        at = pl.ds(c * chunk, chunk)
        outb[c] = jnp.dot(amplitude, rows[:, at], preferred_element_type=f32).astype(bf16)
        pltpu.make_async_copy(outb.at[c], out.at[:, at], out_sem.at[c]).start()
    for c in range(aux // chunk):
        pltpu.make_async_copy(outb.at[c], out.at[:, pl.ds(c * chunk, chunk)], out_sem.at[c]).wait()
    for sent in to_z[1:] + to_x + to_far + to_far_x + far_to_x + to_sib + to_sib_x + mirrors:
        sent.wait_send()


def shards(n_occ, n_vir, orbitals, eps_occ, eps_vir):
    occ_dev, vir_dev, aux = orbitals.shape
    nz = n_vir // 2
    block = n_vir * BATCH_DEV
    chunk = 512
    bf16 = jnp.bfloat16
    count = 7 * nz + 2
    density = pl.pallas_call(
        functools.partial(kernel, n_occ, n_vir),
        out_shape=jax.ShapeDtypeStruct((vir_dev, aux), bf16),
        in_specs=[pl.BlockSpec(memory_space=pl.ANY), pl.BlockSpec(memory_space=pltpu.VMEM),
                  pl.BlockSpec(memory_space=pltpu.VMEM)],
        out_specs=pl.BlockSpec(memory_space=pl.ANY),
        scratch_shapes=[
            pltpu.VMEM((vir_dev, aux), bf16),
            pltpu.VMEM((16, aux), bf16),
            pltpu.VMEM((3, nz, 2, 16, aux // 2 + 128), bf16),
            pltpu.VMEM((3 * block, aux), bf16),
            pltpu.VMEM((2, block, vir_dev), bf16),
            pltpu.VMEM((2, block, vir_dev), bf16),
            pltpu.VMEM((aux // chunk, vir_dev, chunk), bf16),
            pltpu.SemaphoreType.DMA((count,)),
            pltpu.SemaphoreType.DMA((count,)),
            pltpu.SemaphoreType.DMA((2,)),
            pltpu.SemaphoreType.DMA((aux // chunk,)),
        ],
        compiler_params=pltpu.CompilerParams(
            collective_id=0, has_side_effects=True, vmem_limit_bytes=48 * 1024 * 1024),
        name="density",
    )(orbitals.reshape(vir_dev, aux), eps_vir.reshape(1, -1), eps_occ.reshape(1, 1))
    return density.reshape(occ_dev, vir_dev, aux)


def solution(mesh):
    return jax.shard_map(
        functools.partial(shards, mesh.shape["occ"], mesh.shape["vir"]),
        mesh=mesh,
        in_specs=(P("occ", "vir", None), P("occ"), P("vir")),
        out_specs=P("occ", "vir", None),
        check_vma=False,
    )
```

```python
import functools

import jax
import jax.numpy as jnp
from jax import lax
from jax.experimental import pallas as pl
from jax.experimental.pallas import tpu as pltpu
from jax.sharding import PartitionSpec as P

BATCH_DEV = 8
MESH = pl.DeviceIdType.MESH


def kernel(n_occ, n_vir, orb, ev_ref, eo_ref, out, a, head, raw, rows, mir_out, mir_in,
           send_sem, recv_sem, local_sem):
    f32, bf16 = jnp.float32, jnp.bfloat16
    nz = n_vir // 2
    aux = orb.shape[1]
    half = aux // 2
    cut = half // 2
    b = BATCH_DEV
    block = n_vir * b
    o, v = lax.axis_index("occ"), lax.axis_index("vir")
    z, x, core = v // 2, v % 2, o % 2
    along_x = (o, z * 2 + (1 - x))
    sibling = (o + 1 - 2 * core, v)
    far = ((o - 1 + 2 * core + n_occ) % n_occ, v)
    has_up, has_down = z < nz - 1, z > 0
    up, down = (o, v + 2), (o, v - 2)

    inner = jnp.minimum(z, nz - 1 - z)
    order = []
    for k in range(nz):
        near = z - (k + 1) // 2 if k % 2 else z + k // 2
        order.append(jnp.where(k <= 2 * inner, near, jnp.where(2 * z <= nz - 1, k, nz - 1 - k)))

    barrier = pltpu.get_barrier_semaphore()
    for dev in (along_x, sibling, far):
        pl.semaphore_signal(barrier, inc=1, device_id=dev, device_id_type=MESH)

    @pl.when(has_up)
    def _():
        pl.semaphore_signal(barrier, inc=1, device_id=up, device_id_type=MESH)

    @pl.when(has_down)
    def _():
        pl.semaphore_signal(barrier, inc=1, device_id=down, device_id_type=MESH)

    get_head = pltpu.make_async_copy(orb.at[pl.ds(0, 16)], head, local_sem.at[0])
    get_a = pltpu.make_async_copy(orb, a, local_sem.at[1])
    get_head.start()
    get_a.start()
    get_head.wait()

    top = head[...].astype(f32)[0:b]
    raw[0, z, 0, :, 0:half] = jnp.concatenate([top[:, :half], top[:, half:]], axis=0).astype(bf16)
    ev = ev_ref[...].reshape(1, -1).astype(f32)
    lane = lax.broadcasted_iota(jnp.int32, (b, 128), 1)
    row = lax.broadcasted_iota(jnp.int32, (b, 128), 0)
    picked = jnp.where(lane == row, jnp.broadcast_to(ev[:, :128], (b, 128)), 0.0)
    batch_energy = jnp.broadcast_to(jnp.sum(picked, axis=1, keepdims=True), (b, 128))
    occ_energy = jnp.broadcast_to(eo_ref[...].reshape(1, 1).astype(f32), (b, 128))
    raw[0, z, 0, :, half:] = jnp.concatenate([batch_energy, occ_energy], axis=0).astype(bf16)

    parts = (pl.ds(0, cut), pl.ds(cut, half + 128 - cut))

    def copy(kind, s, src, dst, dev, send_kind=None):
        send_kind = kind if send_kind is None else send_kind
        return pltpu.make_async_remote_copy(
            src_ref=src, dst_ref=dst, send_sem=send_sem.at[send_kind, s], recv_sem=recv_sem.at[kind, s],
            device_id=dev, device_id_type=MESH)

    def on_z(s, h, dev, send_kind=None):
        piece = raw.at[0, s, 0, :, parts[h]]
        return copy(h, s, piece, piece, dev, send_kind)

    def on_x(s, h):
        return copy(2 + h, s, raw.at[0, s, 0, :, parts[h]], raw.at[0, s, 1, :, parts[h]], along_x)

    def on_far(s, h):
        return copy(4 + h, s, raw.at[0, s, 0, :, parts[h]], raw.at[2, s, 0, :, parts[h]], far)

    def x_to_far(s):
        return copy(6, s, raw.at[0, s, 1, :, parts[0]], raw.at[2, s, 1, :, parts[0]], far)

    def far_to_x(s):
        return copy(7, s, raw.at[2, s, 0, :, parts[1]], raw.at[2, s, 1, :, parts[1]], along_x)

    def on_sib(s, t):
        return copy(8 + t, s, raw.at[0, s, t], raw.at[1, s, t], sibling)

    early = (nz - 1) * 2 * b

    def mirror(q):
        if q == 0:
            return copy(10, 0, mir_out.at[pl.ds(0, block)], mir_in.at[pl.ds(0, block)], sibling)
        at = pl.ds(block, early) if q == 1 else pl.ds(block + early, block - early)
        return copy(10, q, mir_out.at[at], mir_in.at[at], far)

    def relay(s, h, then):
        @pl.when(jnp.logical_and(s < z, has_up))
        def _():
            then(on_z(s, h, up))

        @pl.when(jnp.logical_and(s > z, has_down))
        def _():
            then(on_z(s, h, down))

    def own_z(h, then):
        @pl.when(has_up)
        def _():
            then(on_z(z, h, up))

        @pl.when(has_down)
        def _():
            then(on_z(z, h, down, 11 + h))

    def unpack(q, k):
        s = order[k]
        p0 = raw[q, s, 0, :, 0:half].astype(f32)
        p1 = raw[q, s, 1, :, 0:half].astype(f32)
        at = pl.ds(q * block + k * 2 * b, 2 * b)
        rows[at, 0:half] = jnp.concatenate([p0[0:b], p1[0:b]], axis=0).astype(bf16)
        rows[at, half:] = jnp.concatenate([p0[b:], p1[b:]], axis=0).astype(bf16)

    pl.semaphore_wait(barrier, 3 + jnp.where(has_up, 1, 0) + jnp.where(has_down, 1, 0))

    def start(c):
        c.start()

    own_z(0, start)
    on_x(z, 0).start()
    on_far(z, 1).start()
    own_z(1, start)
    on_x(z, 1).start()
    on_far(z, 0).start()
    on_sib(z, 0).start()
    for k in range(nz):
        s = order[k]
        if k + 1 < nz:
            following = order[k + 1]
            for h in range(2):
                on_z(following, h, up).wait_recv()
                relay(following, h, start)
                on_x(following, h).start()
                on_far(following, h).start()
            on_sib(following, 0).start()
        on_x(s, 0).wait_recv()
        x_to_far(s).start()
        on_far(s, 1).wait_recv()
        far_to_x(s).start()
        on_x(s, 1).wait_recv()
        on_sib(s, 1).start()
        unpack(0, k)
    get_a.wait()

    def wait_far(k):
        on_far(order[k], 0).wait_recv()
        x_to_far(order[k]).wait_recv()
        far_to_x(order[k]).wait_recv()
        unpack(2, k)

    def coulomb_of(start, size):
        return lax.dot_general(rows[pl.ds(start, size), :], a[...], (((1,), (1,)), ((), ())),
                               preferred_element_type=f32)

    for k in range(nz - 1):
        wait_far(k)
    far_early = coulomb_of(2 * block, early)
    mir_out[pl.ds(block, early), :] = far_early.astype(bf16)
    mirror(1).start()
    for k in range(nz):
        on_sib(order[k], 0).wait_recv()
        on_sib(order[k], 1).wait_recv()
        unpack(1, k)
    near = coulomb_of(0, 2 * block)
    mir_out[pl.ds(0, block), :] = near[block:].astype(bf16)
    mirror(0).start()
    wait_far(nz - 1)
    far_late = coulomb_of(2 * block + early, block - early)
    mir_out[pl.ds(block + early, block - early), :] = far_late.astype(bf16)
    mirror(2).start()

    levels = jnp.concatenate([raw[0, order[k], t, :, half:].astype(f32)[0:b] for k in range(nz) for t in range(2)], axis=0)
    width = a.shape[0]
    reps = width // 128
    levels = jnp.concatenate([levels] * reps, axis=1)

    def occ_of(q):
        return jnp.concatenate([raw[q, z, 0, :, half:].astype(f32)[b:b + 1]] * reps, axis=1)

    base = ev + levels - occ_of(0)
    amp_own = ((2.0 * near[:block] - near[:block]) / (base - occ_of(0))).astype(bf16)
    mirror(0).wait_recv()
    amp_sib = ((2.0 * near[block:] - mir_in[pl.ds(0, block), :].astype(f32)) / (base - occ_of(1))).astype(bf16)
    mirror(1).wait_recv()
    mirror(2).wait_recv()
    far_all = jnp.concatenate([far_early, far_late], axis=0)
    amp_far = ((2.0 * far_all - mir_in[pl.ds(block, block), :].astype(f32)) / (base - occ_of(2))).astype(bf16)
    amplitude = jnp.concatenate([amp_own, amp_sib, amp_far], axis=0).T

    chunk = 512
    for c in range(aux // chunk):
        at = pl.ds(c * chunk, chunk)
        out[:, at] = jnp.dot(amplitude, rows[:, at], preferred_element_type=f32).astype(bf16)

    def finish(c):
        c.wait_send()

    for h in range(2):
        own_z(h, finish)
    for k in range(nz):
        s = order[k]
        for h in range(2):
            if k:
                relay(s, h, finish)
            on_x(s, h).wait_send()
            on_far(s, h).wait_send()
            on_sib(s, h).wait_send()
        x_to_far(s).wait_send()
        far_to_x(s).wait_send()
    for q in range(3):
        mirror(q).wait_send()


def shards(n_occ, n_vir, orbitals, eps_occ, eps_vir):
    occ_dev, vir_dev, aux = orbitals.shape
    nz = n_vir // 2
    block = n_vir * BATCH_DEV
    bf16 = jnp.bfloat16
    density = pl.pallas_call(
        functools.partial(kernel, n_occ, n_vir),
        out_shape=jax.ShapeDtypeStruct((vir_dev, aux), bf16),
        in_specs=[pl.BlockSpec(memory_space=pltpu.HBM), pl.BlockSpec(memory_space=pltpu.VMEM),
                  pl.BlockSpec(memory_space=pltpu.VMEM)],
        out_specs=pl.BlockSpec(memory_space=pltpu.VMEM),
        scratch_shapes=[
            pltpu.VMEM((vir_dev, aux), bf16),
            pltpu.VMEM((16, aux), bf16),
            pltpu.VMEM((3, nz, 2, 16, aux // 2 + 128), bf16),
            pltpu.VMEM((3 * block, aux), bf16),
            pltpu.VMEM((2 * block, vir_dev), bf16),
            pltpu.VMEM((2 * block, vir_dev), bf16),
            pltpu.SemaphoreType.DMA((13, nz)),
            pltpu.SemaphoreType.DMA((11, nz)),
            pltpu.SemaphoreType.DMA((2,)),
        ],
        compiler_params=pltpu.CompilerParams(
            collective_id=0, has_side_effects=True, vmem_limit_bytes=48 * 1024 * 1024),
        name="density",
    )(orbitals.reshape(vir_dev, aux), eps_vir, eps_occ)
    return density.reshape(occ_dev, vir_dev, aux)


def solution(mesh):
    return jax.shard_map(
        functools.partial(shards, mesh.shape["occ"], mesh.shape["vir"]),
        mesh=mesh,
        in_specs=(P("occ", "vir", None), P("occ"), P("vir")),
        out_specs=P("occ", "vir", None),
        check_vma=False,
    )
```

```python
import functools

import jax
import jax.numpy as jnp
from jax import lax
from jax.experimental import pallas as pl
from jax.experimental.pallas import tpu as pltpu
from jax.sharding import PartitionSpec as P

BATCH_DEV = 8
MESH = pl.DeviceIdType.MESH


def kernel(n_occ, n_vir, orb, ev_hbm, eo_ref, amp_ref, rows, a, head, ev_ref, raw, mir_out, mir_in,
           send_sem, recv_sem, local_sem):
    f32, bf16 = jnp.float32, jnp.bfloat16
    nz = n_vir // 2
    aux = orb.shape[1]
    half = aux // 2
    cut = half // 2
    b = BATCH_DEV
    block = n_vir * b
    o, v = lax.axis_index("occ"), lax.axis_index("vir")
    z, x, core = v // 2, v % 2, o % 2
    along_x = (o, z * 2 + (1 - x))
    sibling = (o + 1 - 2 * core, v)
    far = ((o - 1 + 2 * core + n_occ) % n_occ, v)
    inner = jnp.minimum(z, nz - 1 - z)
    order = []
    for k in range(nz):
        near = z - (k + 1) // 2 if k % 2 else z + k // 2
        order.append(jnp.where(k <= 2 * inner, near, jnp.where(2 * z <= nz - 1, k, nz - 1 - k)))

    barrier = pltpu.get_barrier_semaphore()
    for dev in [along_x, sibling, far] + [(o, s * 2 + x) for s in order[1:]]:
        pl.semaphore_signal(barrier, inc=1, device_id=dev, device_id_type=MESH)

    get_head = pltpu.make_async_copy(orb.at[pl.ds(0, 16)], head, local_sem.at[0])
    get_a = pltpu.make_async_copy(orb, a, local_sem.at[1])
    get_ev = pltpu.make_async_copy(ev_hbm, ev_ref, local_sem.at[2])
    get_head.start()
    get_ev.start()
    get_a.start()
    get_head.wait()
    get_ev.wait()

    top = head[...].astype(f32)[0:b]
    raw[0, z, 0, :, 0:half] = jnp.concatenate([top[:, :half], top[:, half:]], axis=0).astype(bf16)
    ev = ev_ref[...].reshape(1, -1).astype(f32)
    lane = lax.broadcasted_iota(jnp.int32, (b, 128), 1)
    row = lax.broadcasted_iota(jnp.int32, (b, 128), 0)
    picked = jnp.where(lane == row, jnp.broadcast_to(ev[:, :128], (b, 128)), 0.0)
    batch_energy = jnp.broadcast_to(jnp.sum(picked, axis=1, keepdims=True), (b, 128))
    occ_energy = jnp.broadcast_to(eo_ref[...].reshape(1, 1).astype(f32), (b, 128))
    raw[0, z, 0, :, half:] = jnp.concatenate([batch_energy, occ_energy], axis=0).astype(bf16)

    parts = (pl.ds(0, cut), pl.ds(cut, half + 128 - cut))

    def copy(kind, s, src, dst, dev, send_at=None):
        return pltpu.make_async_remote_copy(
            src_ref=src, dst_ref=dst, send_sem=send_sem.at[kind, s if send_at is None else send_at],
            recv_sem=recv_sem.at[kind, s], device_id=dev, device_id_type=MESH)

    def to_z(s, h):
        piece = raw.at[0, z, 0, :, parts[h]]
        return copy(h, z, piece, piece, (o, s * 2 + x), s)

    def from_z(s, h):
        piece = raw.at[0, s, 0, :, parts[h]]
        return copy(h, s, piece, piece, (o, s * 2 + x))

    def on_x(s, h):
        return copy(2 + h, s, raw.at[0, s, 0, :, parts[h]], raw.at[0, s, 1, :, parts[h]], along_x)

    def on_far(s, h):
        return copy(4 + h, s, raw.at[0, s, 0, :, parts[h]], raw.at[2, s, 0, :, parts[h]], far)

    def x_to_far(s):
        return copy(6, s, raw.at[0, s, 1, :, parts[0]], raw.at[2, s, 1, :, parts[0]], far)

    def far_to_x(s):
        return copy(7, s, raw.at[2, s, 0, :, parts[1]], raw.at[2, s, 1, :, parts[1]], along_x)

    def on_sib(s, t):
        return copy(8 + t, s, raw.at[0, s, t], raw.at[1, s, t], sibling)

    early = (nz - 1) * 2 * b

    def mirror(q):
        if q == 0:
            return copy(10, 0, mir_out.at[pl.ds(0, block)], mir_in.at[pl.ds(0, block)], sibling)
        at = pl.ds(block, early) if q == 1 else pl.ds(block + early, block - early)
        return copy(10, q, mir_out.at[at], mir_in.at[at], far)

    def unpack(q, k):
        s = order[k]
        p0 = raw[q, s, 0, :, 0:half].astype(f32)
        p1 = raw[q, s, 1, :, 0:half].astype(f32)
        at = pl.ds(q * block + k * 2 * b, 2 * b)
        rows[at, 0:half] = jnp.concatenate([p0[0:b], p1[0:b]], axis=0).astype(bf16)
        rows[at, half:] = jnp.concatenate([p0[b:], p1[b:]], axis=0).astype(bf16)

    pl.semaphore_wait(barrier, nz + 2)
    to_z(order[1], 0).start()
    on_x(z, 0).start()
    on_far(z, 1).start()
    to_z(order[1], 1).start()
    on_x(z, 1).start()
    on_far(z, 0).start()
    for k in range(2, nz):
        to_z(order[k], 0).start()
        to_z(order[k], 1).start()
    on_sib(z, 0).start()
    for k in range(nz):
        s = order[k]
        if k + 1 < nz:
            following = order[k + 1]
            for h in range(2):
                from_z(following, h).wait_recv()
                on_x(following, h).start()
                on_far(following, h).start()
            on_sib(following, 0).start()
        on_x(s, 0).wait_recv()
        x_to_far(s).start()
        on_far(s, 1).wait_recv()
        far_to_x(s).start()
        on_x(s, 1).wait_recv()
        on_sib(s, 1).start()
        unpack(0, k)
    get_a.wait()

    def wait_far(k):
        on_far(order[k], 0).wait_recv()
        x_to_far(order[k]).wait_recv()
        far_to_x(order[k]).wait_recv()
        unpack(2, k)

    def coulomb_of(start, size):
        return lax.dot_general(rows[pl.ds(start, size), :], a[...], (((1,), (1,)), ((), ())),
                               preferred_element_type=f32)

    for k in range(nz - 1):
        wait_far(k)
    far_early = coulomb_of(2 * block, early)
    mir_out[pl.ds(block, early), :] = far_early.astype(bf16)
    mirror(1).start()
    for k in range(nz):
        on_sib(order[k], 0).wait_recv()
        on_sib(order[k], 1).wait_recv()
        unpack(1, k)
    near = coulomb_of(0, 2 * block)
    mir_out[pl.ds(0, block), :] = near[block:].astype(bf16)
    mirror(0).start()
    wait_far(nz - 1)
    far_late = coulomb_of(2 * block + early, block - early)
    mir_out[pl.ds(block + early, block - early), :] = far_late.astype(bf16)
    mirror(2).start()

    levels = jnp.concatenate([raw[0, order[k], t, :, half:].astype(f32)[0:b] for k in range(nz) for t in range(2)], axis=0)
    width = a.shape[0]
    reps = width // 128
    levels = jnp.concatenate([levels] * reps, axis=1)

    def occ_of(q):
        return jnp.concatenate([raw[q, z, 0, :, half:].astype(f32)[b:b + 1]] * reps, axis=1)

    base = ev + levels - occ_of(0)
    amp_own = ((2.0 * near[:block] - near[:block]) / (base - occ_of(0))).astype(bf16)
    mirror(0).wait_recv()
    amp_sib = ((2.0 * near[block:] - mir_in[pl.ds(0, block), :].astype(f32)) / (base - occ_of(1))).astype(bf16)
    mirror(1).wait_recv()
    mirror(2).wait_recv()
    far_all = jnp.concatenate([far_early, far_late], axis=0)
    amp_far = ((2.0 * far_all - mir_in[pl.ds(block, block), :].astype(f32)) / (base - occ_of(2))).astype(bf16)
    amp_ref[...] = jnp.concatenate([amp_own, amp_sib, amp_far], axis=0).T

    for k in range(nz):
        s = order[k]
        for h in range(2):
            if k:
                to_z(s, h).wait_send()
            on_x(s, h).wait_send()
            on_far(s, h).wait_send()
            on_sib(s, h).wait_send()
        x_to_far(s).wait_send()
        far_to_x(s).wait_send()
    for q in range(3):
        mirror(q).wait_send()


def shards(n_occ, n_vir, orbitals, eps_occ, eps_vir):
    occ_dev, vir_dev, aux = orbitals.shape
    nz = n_vir // 2
    block = n_vir * BATCH_DEV
    bf16 = jnp.bfloat16
    amplitude, rows = pl.pallas_call(
        functools.partial(kernel, n_occ, n_vir),
        out_shape=(jax.ShapeDtypeStruct((vir_dev, 3 * block), bf16), jax.ShapeDtypeStruct((3 * block, aux), bf16)),
        in_specs=[pl.BlockSpec(memory_space=pltpu.HBM), pl.BlockSpec(memory_space=pltpu.HBM),
                  pl.BlockSpec(memory_space=pltpu.VMEM)],
        out_specs=[pl.BlockSpec(memory_space=pltpu.VMEM)] * 2,
        scratch_shapes=[
            pltpu.VMEM((vir_dev, aux), bf16),
            pltpu.VMEM((16, aux), bf16),
            pltpu.VMEM((vir_dev,), bf16),
            pltpu.VMEM((3, nz, 2, 16, aux // 2 + 128), bf16),
            pltpu.VMEM((2 * block, vir_dev), bf16),
            pltpu.VMEM((2 * block, vir_dev), bf16),
            pltpu.SemaphoreType.DMA((11, nz)),
            pltpu.SemaphoreType.DMA((11, nz)),
            pltpu.SemaphoreType.DMA((3,)),
        ],
        compiler_params=pltpu.CompilerParams(
            collective_id=0, has_side_effects=True, vmem_limit_bytes=51 * 1024 * 1024),
        name="amplitude",
    )(orbitals.reshape(vir_dev, aux), eps_vir, eps_occ)
    density = jnp.dot(amplitude, rows, preferred_element_type=jnp.float32).astype(bf16)
    return density.reshape(occ_dev, vir_dev, aux)


def solution(mesh):
    return jax.shard_map(
        functools.partial(shards, mesh.shape["occ"], mesh.shape["vir"]),
        mesh=mesh,
        in_specs=(P("occ", "vir", None), P("occ"), P("vir")),
        out_specs=P("occ", "vir", None),
        check_vma=False,
    )
```
